32 devices in a mesh: groups: 2 (over x), tensor: 16 (over z, y, core).
Axes of the slice: x: 2, y: 2, z: 4, core: 2. Of those that a mesh axis runs over, the one named last changes fastest.
Arguments:
- residual_input: bfloat16 [2, 512, 8192], P(None, 'groups', 'tensor'), parts along dimension 1, may hold values from -6 to 6
- gain: bfloat16 [8192], P('tensor'), may hold values from 0.099609375 to 1.8984375
- gate_up_weight: bfloat16 [8192, 2, 14336], P(None, None, 'tensor'), may hold values from -0.0625 to 0.0625
- adapter_down_maps: bfloat16 [8192, 16, 128], P('tensor'), may hold values from -0.0625 to 0.0625
- adapter_up_maps: bfloat16 [16, 2, 64, 14336], P('tensor'), may hold values from -0.75 to 0.75
- row_adapter_index: int32 [2, 512, 1], P(None, 'groups'), parts along dimension 1, may hold values from 0 to 15; in each aligned block of 256 rows (0 to 255, 256 to 511, ..., all dimensions but the last counted through in order) at most 16 rows name the same one
- adapter_storage_slot: int32 [16], replicated, may hold values from 0 to 15, each once
Outputs:
- hidden_out: bfloat16 [2, 512, 14336], P(None, 'groups', 'tensor'), parts along dimension 1
The draws below stay inside these ranges and needn't reach their ends.
There are 2 independent parts, one for each index of `groups`. The reference program is written for one: setup_inputs(seed, part) draws one part's arguments, and reference() takes and returns one part's arrays. A program takes and returns all parts, laid end to end along the dimension named above; an argument that names none is the same for every part. Nothing has to cross between parts.
Inputs may be any that keep to these rules, and one draw needn't show every extreme that they name: `row_adapter_index`: within one decode step at most 16 rows name the same adapter, and in some step one adapter is named by exactly 16 rows. `adapter_storage_slot`: each slot is used by exactly one adapter.
All inputs are finite; a program needn't handle non-finite values.
Results may differ from the reference program's by a relative error of at most 0.0079.
Values may be sent and summed in bfloat16 or wider, within the bound.
A program may use at most 256 MiB of HBM per device.

```python
import math
import jax
import jax.numpy as jnp
import numpy as np
from jax import lax

MODEL_WIDTH = 8192
HIDDEN_UNITS = 14336
ADAPTER_RANK = 64
STEPS = 2
ROWS = 256
ADAPTER_COUNT = 16
CAP = 16


def levels(stream_key, dims, shards, least, largest):
    def one(position, blocks):
        heights = jax.random.uniform(jax.random.fold_in(jax.random.fold_in(stream_key, 6), position), (blocks,), jnp.float32, least / len(shards), largest / len(shards))
        return jnp.repeat(jnp.exp(heights), dims[position] // blocks).reshape((-1,) + (1,) * (len(dims) - position - 1))

    factor_of = one(*shards[0])
    for cut in shards[1:]:
        factor_of = factor_of * one(*cut)
    return factor_of


def deal_out(stream_key, own, number, rows, amount, top, limit, lean):
    sequence = jax.random.permutation(stream_key, amount)
    packed, common = shares(amount, rows * top, limit, lean, True), shares(amount, rows * top, limit, lean, False)
    places = jnp.arange(amount)

    def named(lengths, turn):
        used = int((lengths > 0).sum())
        fixed = max(1, used // 4)
        shifted = fixed + (places - fixed + turn * (used - fixed)) % max(1, amount - fixed)
        return jnp.zeros((amount,), jnp.int32).at[sequence[jnp.where(places < fixed, places, shifted)]].set(jnp.asarray(lengths, jnp.int32))

    lengths = jnp.where(number % 4 == 0, named(packed, number // 4), named(common, number - number // 4 - 1))
    mixed = jax.random.permutation(jax.random.fold_in(own, 3), amount)
    giver, taker = mixed[0:amount // 2 * 2:2], mixed[1:amount // 2 * 2:2]
    margin = jnp.minimum(lengths[giver] - 1, limit - lengths[taker]) // 2
    margin = jnp.where((giver == sequence[0]) | (taker == sequence[0]) | (lengths[taker] == 0), 0, jnp.maximum(margin, 0))
    shifted = jax.random.randint(jax.random.fold_in(own, 4), (amount // 2,), 0, 1 << 20) % (margin + 1)
    lengths = lengths.at[giver].add(-shifted).at[taker].add(shifted)
    labels = jnp.searchsorted(jnp.cumsum(lengths), jnp.arange(rows * top), side="right").astype(jnp.int32)
    table = labels.reshape(top, rows).T
    table = table[jax.random.permutation(jax.random.fold_in(own, 1), rows)]
    turn = jax.random.randint(jax.random.fold_in(own, 2), (rows, 1), 0, top)
    return jnp.take_along_axis(table, (jnp.arange(top)[None, :] + turn) % top, axis=1)


def shares(amount, total, reach, lean, full):
    portions = [(1 << 20) // math.isqrt(rank ** lean) + 1 for rank in range(1, amount + 1)]
    largest = reach if full else min(reach, max(-(-total // amount), total * portions[0] // sum(portions)))
    least = 1 if total - largest >= amount - 1 else 0
    holding, surplus = [largest] + [least] * (amount - 1), total - largest - least * (amount - 1)
    while surplus > 0:
        candidates = [i for i in range(1, amount) if holding[i] < largest] or [i for i in range(1, amount) if holding[i] < reach]
        pool, remaining = sum([portions[i] for i in candidates]), surplus
        for i in candidates:
            more = min(reach - holding[i], max(1, remaining * portions[i] // pool), surplus)
            holding[i] = holding[i] + more
            surplus = surplus - more
    return np.array(holding)


def centred(own_key, shape, scale, limit, split=(), dtype=jnp.bfloat16):
    values = scale * jax.random.normal(own_key, shape, jnp.float32)
    if split:
        values = values * levels(own_key, shape, split, -0.22, 0.18)
    return jnp.clip(values, -limit, limit).astype(dtype)


def setup_inputs(seed: int = 0, part: int = 0) -> dict:
    keys = jax.random.split(jax.random.key(seed), 8)
    part_splits = jax.random.split(jax.random.fold_in(keys[7], part), 8)
    residual_input = centred(part_splits[0], (STEPS, ROWS, MODEL_WIDTH), 1.0, 6.0, ((2, 16),))
    gain = jnp.clip(1.0 + 0.18 * jax.random.normal(keys[1], (MODEL_WIDTH,), jnp.float32), 0.099609375, 1.8984375).astype(jnp.bfloat16)
    gate_up_weight = centred(keys[2], (MODEL_WIDTH, 2, HIDDEN_UNITS), MODEL_WIDTH ** -0.5, 0.0625, ((2, 16),))
    adapter_down_maps = centred(keys[3], (MODEL_WIDTH, ADAPTER_COUNT, 2 * ADAPTER_RANK), MODEL_WIDTH ** -0.5, 0.0625, ((0, 16),))
    adapter_up_maps = centred(keys[4], (ADAPTER_COUNT, 2, ADAPTER_RANK, HIDDEN_UNITS), ADAPTER_RANK ** -0.5, 0.75, ((0, 16),))
    row_adapter_index_keys = jax.random.split(jax.random.fold_in(part_splits[5], 1), STEPS * ROWS // ROWS)
    row_adapter_index_turns = jax.random.permutation(jax.random.fold_in(part_splits[5], 3), STEPS * ROWS // ROWS)
    row_adapter_index = jax.vmap(lambda own, number: deal_out(jax.random.fold_in(part_splits[5], 2), own, number, ROWS, ADAPTER_COUNT, 1, CAP, 2))(row_adapter_index_keys, row_adapter_index_turns).reshape((STEPS, ROWS, 1))
    adapter_storage_slot = jax.random.permutation(keys[6], ADAPTER_COUNT).astype(jnp.int32)
    return {"residual_input": residual_input, "gain": gain, "gate_up_weight": gate_up_weight, "adapter_down_maps": adapter_down_maps, "adapter_up_maps": adapter_up_maps, "row_adapter_index": row_adapter_index, "adapter_storage_slot": adapter_storage_slot}


def reference(residual_input, gain, gate_up_weight, adapter_down_maps, adapter_up_maps, row_adapter_index, adapter_storage_slot):
    flat = residual_input.reshape(STEPS * ROWS, MODEL_WIDTH).astype(jnp.float32)
    rstd = lax.rsqrt(lax.optimization_barrier(jnp.mean(flat * flat, axis=1, keepdims=True)) + 1e-05)
    normed_input = (flat * rstd * gain.astype(jnp.float32)).astype(jnp.bfloat16)
    base_output = jnp.dot(normed_input, gate_up_weight.reshape(MODEL_WIDTH, 2 * HIDDEN_UNITS), preferred_element_type=jnp.float32)
    base_output = base_output.reshape(STEPS * ROWS, 2, HIDDEN_UNITS)
    ids = row_adapter_index.reshape(STEPS * ROWS).astype(jnp.int32)
    every_slot = jnp.dot(normed_input, adapter_down_maps.reshape(MODEL_WIDTH, ADAPTER_COUNT * 2 * ADAPTER_RANK), preferred_element_type=jnp.float32)
    every_slot = every_slot.reshape(STEPS * ROWS, ADAPTER_COUNT, 2 * ADAPTER_RANK)
    shrink_output = jnp.take_along_axis(every_slot, ids[:, None, None], axis=1)[:, 0, :].astype(jnp.bfloat16)
    storage_slot = adapter_storage_slot[ids].astype(jnp.int32)

    def single_row(pair):
        values, select_where = pair
        slot_maps = lax.dynamic_index_in_dim(adapter_up_maps, select_where, 0, keepdims=False)
        gate_term = jnp.dot(values[:ADAPTER_RANK], slot_maps[0], preferred_element_type=jnp.float32)
        up_term = jnp.dot(values[ADAPTER_RANK:], slot_maps[1], preferred_element_type=jnp.float32)
        return jnp.stack([gate_term, up_term], axis=0).astype(jnp.bfloat16)
    adapter_output = lax.map(single_row, (shrink_output, storage_slot)).astype(jnp.float32)
    gate_output = base_output[:, 0, :] + 2.0 * adapter_output[:, 0, :]
    upper_output = base_output[:, 1, :] + 2.0 * adapter_output[:, 1, :]
    result = (jax.nn.silu(gate_output) * upper_output).astype(jnp.bfloat16)
    return result.reshape(STEPS, ROWS, HIDDEN_UNITS)
```

```python
import functools
import jax
import jax.numpy as jnp
from jax import lax
from jax.experimental import pallas as pl
from jax.experimental.pallas import tpu as pltpu
from jax.sharding import PartitionSpec as P

CAP = 16
MESH = pl.DeviceIdType.MESH


def exchange(n, ny, lf, wide, xg, ssq, sp, up, xall, ssq_all, lora_all,
             sp_all, lora_buf, x_send, x_recv, q_send, q_recv, s_send, s_recv,
             l_send, l_recv, own_sem):
    nz = n // (2 * ny)
    me = lax.axis_index("tensor")
    core = lax.rem(me, 2)
    y = lax.rem(me // 2, ny)
    z = me // (2 * ny)
    half = up.shape[-2]

    def index(zz, yy, cc):
        return (zz * ny + yy) * 2 + cc

    barrier = pltpu.get_barrier_semaphore()

    @pl.loop(1, n)
    def _(d):
        pl.semaphore_signal(barrier, inc=1, device_id={"tensor": lax.rem(me + d, n)},
                            device_id_type=MESH)

    pl.semaphore_wait(barrier, n - 1)

    def remote(src, dst, send, recv, peer):
        return pltpu.make_async_remote_copy(
            src_ref=src, dst_ref=dst, send_sem=send, recv_sem=recv,
            device_id={"tensor": peer}, device_id_type=MESH)

    def sp_copy(peer, slot):
        return remote(sp.at[peer], sp_all.at[slot], s_send.at[peer], s_recv.at[slot], peer)

    def ssq_copy(peer, slot):
        return remote(ssq, ssq_all.at[slot], q_send.at[peer], q_recv.at[slot], peer)

    def lora_copy(peer, slot):
        return remote(lora_buf.at[peer], lora_all.at[slot], l_send.at[peer],
                      l_recv.at[slot], peer)

    def x_copy(src, way, block, peer):
        return remote(src, xall.at[block], x_send.at[way, block], x_recv.at[block], peer)

    def sends(block, src, act, up_way, down_way, y_way):
        if up_way is not None:
            @pl.when(jnp.logical_and(up_way, z + 1 < nz))
            def _():
                act(x_copy(src, 0, block, lax.rem(index(z + 1, y, core), n)))
        if down_way is not None:
            @pl.when(jnp.logical_and(down_way, z > 0))
            def _():
                act(x_copy(src, 1, block, lax.rem(index(z - 1, y, core) + n, n)))
        if y_way and ny == 2:
            act(x_copy(src, 2, block, index(z, 1 - y, core)))
        act(x_copy(src, 3, block, index(z, y, 1 - core)))

    def begin(copy):
        copy.start()

    @pl.loop(1, n)
    def _(d):
        sp_copy(lax.rem(me + d, n), me).start()

    yes = z >= 0
    sends(me, xg, begin, yes, yes, True)

    @pl.loop(1, n)
    def _(d):
        ssq_copy(lax.rem(me + d, n), me).start()

    own = [pltpu.make_async_copy(sp.at[me], sp_all.at[me], own_sem.at[0]),
           pltpu.make_async_copy(ssq, ssq_all.at[me], own_sem.at[1]),
           pltpu.make_async_copy(xg, xall.at[me], own_sem.at[2])]
    for copy in own:
        copy.start()
    own[0].wait()

    @pl.loop(1, n)
    def _(d):
        peer = lax.rem(me + d, n)
        sp_copy(peer, peer).wait_recv()

    shrink = jnp.sum(sp_all[...], axis=0).astype(jnp.bfloat16)

    @pl.loop(1, n + 1)
    def _(d):
        peer = lax.rem(me + d, n)
        for g in range(2):
            if wide:
                maps = up[0, g, :, pl.ds(pl.multiple_of(peer * lf, 128), lf)]
            else:
                maps = up[peer, g]
            lora_buf[peer, g] = jnp.dot(
                shrink[:, g * half:(g + 1) * half], maps,
                preferred_element_type=jnp.float32).astype(jnp.bfloat16)

        @pl.when(d < n)
        def _():
            lora_copy(peer, me).start()

    mine = pltpu.make_async_copy(lora_buf.at[me], lora_all.at[me], own_sem.at[3])
    mine.start()

    def landed(block):
        x_copy(xall.at[block], 0, block, lax.rem(me + 1, n)).wait_recv()

    def from_line(step, act, wait):
        @pl.when(z - step >= 0)
        def _():
            block = lax.rem(index(z - step, y, core) + n, n)
            if wait:
                landed(block)
            sends(block, xall.at[block], act, yes, None, True)

        @pl.when(z + step < nz)
        def _():
            block = lax.rem(index(z + step, y, core), n)
            if wait:
                landed(block)
            sends(block, xall.at[block], act, None, yes, True)

    def from_side(zz, act, wait):
        block = lax.rem(index(zz, 1 - y, core) + n, n)
        if wait:
            landed(block)
        act(x_copy(xall.at[block], 3, block, index(z, y, 1 - core)))

    def from_sides(step, act, wait):
        @pl.when(z - step >= 0)
        def _():
            from_side(z - step, act, wait)

        @pl.when(z + step < nz)
        def _():
            from_side(z + step, act, wait)

    @pl.loop(1, nz)
    def _(step):
        from_line(step, begin, True)
        if ny == 2:
            @pl.when(step == 1)
            def _():
                from_side(z, begin, True)

            @pl.when(step > 1)
            def _():
                from_sides(step - 1, begin, True)

    if ny == 2:
        from_sides(nz - 1, begin, True)

    @pl.loop(0, n // 2)
    def _(pair):
        landed(pair * 2 + 1 - core)

    @pl.loop(1, n)
    def _(d):
        peer = lax.rem(me + d, n)
        lora_copy(peer, peer).wait_recv()
        ssq_copy(peer, peer).wait_recv()
        lora_copy(peer, me).wait_send()
        ssq_copy(peer, me).wait_send()
        sp_copy(peer, me).wait_send()

    def finish(copy):
        copy.wait_send()

    sends(me, xg, finish, yes, yes, True)
    if ny == 2:
        from_side(z, finish, False)

    @pl.loop(1, nz)
    def _(step):
        from_line(step, finish, False)
        if ny == 2:
            from_sides(step, finish, False)

    own[1].wait()
    own[2].wait()
    mine.wait()


def project(n, x, w, back, lora, rstd, out, acc):
    k = pl.program_id(0)

    @pl.when(k == 0)
    def _():
        for g in range(2):
            rows = lora[:, g].reshape(lora.shape[0] * lora.shape[2], lora.shape[3])
            acc[g] = 2.0 * jnp.dot(back[...], rows, preferred_element_type=jnp.float32)

    for g in range(2):
        acc[g] += jnp.dot(x[0], w[g], preferred_element_type=jnp.float32)

    @pl.when(k == n - 1)
    def _():
        gate = acc[0] * rstd[...]
        upper = acc[1] * rstd[...]
        out[...] = (gate / (1.0 + jnp.exp(-gate)) * upper).astype(out.dtype)


def per_device(n, x, gain, weight, down, up, row_ids, slots):
    steps, rows, width = x.shape
    lf = weight.shape[2]
    total = steps * rows
    adapters, paired = down.shape[1], down.shape[2]
    rank = paired // 2
    block = steps * CAP
    ny = 2 if n == 16 else 1
    flat = x.reshape(total, width).astype(jnp.float32)
    xg = (flat * gain.astype(jnp.float32)[None, :]).astype(jnp.bfloat16)
    ssq = jnp.sum(flat * flat, axis=1).reshape(total // 128, 128)
    ssq = jnp.pad(ssq, ((0, 8 - total // 128), (0, 0)))

    ids = row_ids.reshape(steps, rows)
    earlier = jnp.arange(rows)[None, :] < jnp.arange(rows)[:, None]
    same = jnp.logical_and(ids[:, :, None] == ids[:, None, :], earlier[None])
    place = jnp.sum(same.astype(jnp.int32), axis=2) + CAP * jnp.arange(steps, dtype=jnp.int32)[:, None]
    place = place.reshape(total)
    ids = ids.reshape(total)
    hot = ids[:, None] == jnp.arange(adapters, dtype=jnp.int32)[None, :]
    slot = jnp.sum(jnp.where(hot, slots[None, :], 0), axis=1)
    spots = jnp.arange(adapters * block, dtype=jnp.int32)
    out_map = (spots[:, None] == (ids * block + place)[None, :]).astype(jnp.bfloat16)
    back = ((slot * block + place)[:, None] == spots[None, :]).astype(jnp.bfloat16)
    sent = jnp.dot(out_map, xg, preferred_element_type=jnp.float32).astype(jnp.bfloat16)
    sp = jnp.einsum("apk,kac->apc", sent.reshape(adapters, block, width), down,
                    preferred_element_type=jnp.float32)
    order = (jnp.arange(adapters, dtype=jnp.int32)[:, None] == slots[None, :]).astype(jnp.float32)
    sp = jnp.einsum("ta,apc->tpc", order, sp, precision=lax.Precision.HIGHEST)

    wide = lf % 128 == 0
    maps = up if wide else up.reshape(2, rank, n, lf).transpose(2, 0, 1, 3)
    vmem = pl.BlockSpec(memory_space=pltpu.VMEM)
    hbm = pl.BlockSpec(memory_space=pl.ANY)
    dma = pltpu.SemaphoreType.DMA
    xall, ssq_all, lora = pl.pallas_call(
        functools.partial(exchange, n, ny, lf, wide),
        out_shape=(
            jax.ShapeDtypeStruct((n, total, width), jnp.bfloat16),
            jax.ShapeDtypeStruct((n, 8, 128), jnp.float32),
            jax.ShapeDtypeStruct((n, 2, block, lf), jnp.bfloat16),
        ),
        in_specs=[vmem] * 4,
        out_specs=(hbm, vmem, vmem),
        scratch_shapes=[
            pltpu.VMEM((n, block, paired), jnp.float32),
            pltpu.VMEM((n, 2, block, lf), jnp.bfloat16),
            dma((4, n)), dma((n,)), dma((n,)), dma((n,)), dma((n,)), dma((n,)),
            dma((n,)), dma((n,)), dma((4,)),
        ],
        compiler_params=pltpu.CompilerParams(
            collective_id=0, has_side_effects=True, vmem_limit_bytes=40 * 2**20),
    )(xg, ssq, sp, maps)
    sums = jnp.sum(ssq_all, axis=0)[: total // 128].reshape(total, 1)
    rstd = lax.rsqrt(sums / (width * n) + 1e-05)
    apart = weight.transpose(1, 0, 2)
    out = pl.pallas_call(
        functools.partial(project, n),
        grid=(n,),
        out_shape=jax.ShapeDtypeStruct((total, lf), jnp.bfloat16),
        in_specs=[
            pl.BlockSpec((1, total, width), lambda k: (k, 0, 0)),
            pl.BlockSpec((2, width, lf), lambda k: (0, k, 0)),
            vmem, vmem, vmem,
        ],
        out_specs=pl.BlockSpec((total, lf), lambda k: (0, 0)),
        scratch_shapes=[pltpu.VMEM((2, total, lf), jnp.float32)],
        compiler_params=pltpu.CompilerParams(vmem_limit_bytes=48 * 2**20),
    )(xall, apart, back, lora, rstd)
    return out.reshape(steps, rows, lf)


def solution(mesh):
    return jax.shard_map(
        functools.partial(per_device, mesh.shape["tensor"]),
        mesh=mesh,
        in_specs=(
            P(None, "groups", "tensor"),
            P("tensor"),
            P(None, None, "tensor"),
            P("tensor", None, None),
            P("tensor", None, None, None),
            P(None, "groups", None),
            P(),
        ),
        out_specs=P(None, "groups", "tensor"),
        check_vma=False,
    )
```

```python
import functools
import jax
import jax.numpy as jnp
from jax import lax
from jax.experimental import pallas as pl
from jax.experimental.pallas import tpu as pltpu
from jax.sharding import PartitionSpec as P

CAP = 16
MESH = pl.DeviceIdType.MESH


def exchange(n, ny, lf, wide, xg, ssq, sp, up, back, weight, out, xall, ssq_all,
             lora_all, sp_all, lora_buf, w, acc, x_send, x_recv, q_send, q_recv,
             s_send, s_recv, l_send, l_recv, own_sem):
    nz = n // (2 * ny)
    me = lax.axis_index("tensor")
    core = lax.rem(me, 2)
    y = lax.rem(me // 2, ny)
    z = me // (2 * ny)
    half = up.shape[-2]
    total, width = xg.shape
    part = total // 2

    def index(zz, yy, cc):
        return lax.rem((zz * ny + yy) * 2 + cc + n, n)

    load = pltpu.make_async_copy(weight, w, own_sem.at[2])
    load.start()

    barrier = pltpu.get_barrier_semaphore()

    @pl.loop(1, n)
    def _(d):
        pl.semaphore_signal(barrier, inc=1, device_id={"tensor": lax.rem(me + d, n)},
                            device_id_type=MESH)

    pl.semaphore_wait(barrier, n - 1)

    def remote(src, dst, send, recv, peer):
        return pltpu.make_async_remote_copy(
            src_ref=src, dst_ref=dst, send_sem=send, recv_sem=recv,
            device_id={"tensor": peer}, device_id_type=MESH)

    def sp_copy(peer, slot):
        return remote(sp.at[peer], sp_all.at[slot], s_send.at[peer], s_recv.at[slot], peer)

    def ssq_copy(peer, slot):
        return remote(ssq, ssq_all.at[slot], q_send.at[peer], q_recv.at[slot], peer)

    def lora_copy(peer, slot):
        return remote(lora_buf.at[peer], lora_all.at[slot], l_send.at[peer],
                      l_recv.at[slot], peer)

    def rows(h):
        return pl.ds(h * part, part)

    def x_copy(own, way, block, h, peer):
        src = xg.at[rows(h)] if own else xall.at[block, rows(h)]
        return remote(src, xall.at[block, rows(h)], x_send.at[way, block, h],
                      x_recv.at[block, h], peer)

    def sends(block, h, own, act, rising, falling, across):
        if rising:
            @pl.when(z + 1 < nz)
            def _():
                act(x_copy(own, 0, block, h, index(z + 1, y, core)))
        if falling:
            @pl.when(z > 0)
            def _():
                act(x_copy(own, 1, block, h, index(z - 1, y, core)))
        if across and ny == 2:
            act(x_copy(own, 2, block, h, index(z, 1 - y, core)))
        act(x_copy(own, 3, block, h, index(z, y, 1 - core)))

    def landed(block, h):
        x_copy(False, 0, block, h, lax.rem(me + 1, n)).wait_recv()

    def both(step, run):
        @pl.when(jnp.logical_and(step >= 0, z - step >= 0))
        def _():
            run(z - step, True)

        @pl.when(jnp.logical_and(step > 0, z + step < nz))
        def _():
            run(z + step, False)

    def relay(step, act, wait):
        for h in range(2):
            def line(zz, rising):
                block = index(zz, y, core)
                if wait:
                    landed(block, h)
                sends(block, h, False, act, rising, not rising, True)

            both(step, line)

    def relay_side(step, act, wait):
        for h in range(2):
            def side(zz, rising):
                block = index(zz, 1 - y, core)
                if wait:
                    landed(block, h)
                act(x_copy(False, 3, block, h, index(z, y, 1 - core)))

            both(step, side)

    def use(step, yy, cc, wait):
        def one(zz, rising):
            block = index(zz, yy, cc)
            if wait:
                landed(block, 0)
                landed(block, 1)
            for g in range(2):
                acc[g] += jnp.dot(xall[block], w[g, pl.ds(pl.multiple_of(block * width, 128), width)],
                                  preferred_element_type=jnp.float32)

        both(step, one)

    def begin(copy):
        copy.start()

    def finish(copy):
        copy.wait_send()

    @pl.loop(1, n)
    def _(d):
        sp_copy(lax.rem(me + d, n), me).start()

    for h in range(2):
        sends(me, h, True, begin, True, True, True)

    @pl.loop(1, n)
    def _(d):
        ssq_copy(lax.rem(me + d, n), me).start()

    own = [pltpu.make_async_copy(sp.at[me], sp_all.at[me], own_sem.at[0]),
           pltpu.make_async_copy(ssq, ssq_all.at[me], own_sem.at[1])]
    for copy in own:
        copy.start()
    own[0].wait()

    @pl.loop(1, n)
    def _(d):
        peer = lax.rem(me + d, n)
        sp_copy(peer, peer).wait_recv()

    shrink = jnp.sum(sp_all[...], axis=0).astype(jnp.bfloat16)

    @pl.loop(1, n + 1)
    def _(d):
        peer = lax.rem(me + d, n)
        for g in range(2):
            if wide:
                maps = up[0, g, :, pl.ds(pl.multiple_of(peer * lf, 128), lf)]
            else:
                maps = up[peer, g]
            lora_buf[peer, g] = jnp.dot(
                shrink[:, g * half:(g + 1) * half], maps,
                preferred_element_type=jnp.float32).astype(jnp.bfloat16)

        @pl.when(d < n)
        def _():
            lora_copy(peer, me).start()

    mine = pltpu.make_async_copy(lora_buf.at[me], lora_all.at[me], own_sem.at[3])
    mine.start()

    load.wait()
    for g in range(2):
        acc[g] = jnp.dot(xg[...], w[g, pl.ds(pl.multiple_of(me * width, 128), width)],
                         preferred_element_type=jnp.float32)

    @pl.loop(1, nz)
    def _(step):
        relay(step, begin, True)
        if ny == 2:
            relay_side(step - 1, begin, True)
        use(step, y, core, False)
        use(step - 1, y, 1 - core, True)
        if ny == 2:
            use(step - 1, 1 - y, core, False)
            use(step - 2, 1 - y, 1 - core, True)

    if ny == 2:
        relay_side(nz - 1, begin, True)
        use(nz - 1, 1 - y, core, False)
        use(nz - 2, 1 - y, 1 - core, True)
    use(nz - 1, y, 1 - core, True)

    @pl.loop(1, n)
    def _(d):
        peer = lax.rem(me + d, n)
        lora_copy(peer, peer).wait_recv()
        ssq_copy(peer, peer).wait_recv()

    own[1].wait()
    mine.wait()
    for g in range(2):
        flat = lora_all[:, g].reshape(back.shape[1], lf)
        acc[g] += 2.0 * jnp.dot(back[...], flat, preferred_element_type=jnp.float32)
    if ny == 2:
        use(nz - 1, 1 - y, 1 - core, True)

    sums = jnp.sum(ssq_all[...], axis=0)
    diagonal = (lax.broadcasted_iota(jnp.int32, (128, 128), 0)
                == lax.broadcasted_iota(jnp.int32, (128, 128), 1))
    for i in range(total // 128):
        line = jnp.broadcast_to(sums[i:i + 1, :], (128, 128))
        column = jnp.sum(jnp.where(diagonal, line, 0.0), axis=1, keepdims=True)
        rstd = lax.rsqrt(column / (width * n) + 1e-05)
        gate = acc[0, i * 128:(i + 1) * 128] * rstd
        upper = acc[1, i * 128:(i + 1) * 128] * rstd
        out[i * 128:(i + 1) * 128, :] = (
            gate / (1.0 + jnp.exp(-gate)) * upper).astype(out.dtype)

    @pl.loop(1, n)
    def _(d):
        peer = lax.rem(me + d, n)
        lora_copy(peer, me).wait_send()
        ssq_copy(peer, me).wait_send()
        sp_copy(peer, me).wait_send()

    for h in range(2):
        sends(me, h, True, finish, True, True, True)

    @pl.loop(1, nz)
    def _(step):
        relay(step, finish, False)

    if ny == 2:
        @pl.loop(0, nz)
        def _(step):
            relay_side(step, finish, False)


def per_device(n, x, gain, weight, down, up, row_ids, slots):
    steps, rows, width = x.shape
    lf = weight.shape[2]
    total = steps * rows
    adapters, paired = down.shape[1], down.shape[2]
    rank = paired // 2
    block = steps * CAP
    ny = 2 if n == 16 else 1
    flat = x.reshape(total, width).astype(jnp.float32)
    xg = (flat * gain.astype(jnp.float32)[None, :]).astype(jnp.bfloat16)
    ssq = jnp.sum(flat * flat, axis=1).reshape(total // 128, 128)
    ssq = jnp.pad(ssq, ((0, 8 - total // 128), (0, 0)))

    ids = row_ids.reshape(steps, rows)
    earlier = jnp.arange(rows)[None, :] < jnp.arange(rows)[:, None]
    same = jnp.logical_and(ids[:, :, None] == ids[:, None, :], earlier[None])
    place = jnp.sum(same.astype(jnp.int32), axis=2) + CAP * jnp.arange(steps, dtype=jnp.int32)[:, None]
    place = place.reshape(total)
    ids = ids.reshape(total)
    hot = ids[:, None] == jnp.arange(adapters, dtype=jnp.int32)[None, :]
    slot = jnp.sum(jnp.where(hot, slots[None, :], 0), axis=1)
    spots = jnp.arange(adapters * block, dtype=jnp.int32)
    out_map = (spots[:, None] == (ids * block + place)[None, :]).astype(jnp.bfloat16)
    back = ((slot * block + place)[:, None] == spots[None, :]).astype(jnp.bfloat16)
    sent = jnp.dot(out_map, xg, preferred_element_type=jnp.float32).astype(jnp.bfloat16)
    sp = jnp.einsum("apk,kac->apc", sent.reshape(adapters, block, width), down,
                    preferred_element_type=jnp.float32)
    order = (jnp.arange(adapters, dtype=jnp.int32)[:, None] == slots[None, :]).astype(jnp.float32)
    sp = jnp.einsum("ta,apc->tpc", order, sp, precision=lax.Precision.HIGHEST)

    wide = lf % 128 == 0
    maps = up if wide else up.reshape(2, rank, n, lf).transpose(2, 0, 1, 3)
    vmem = pl.BlockSpec(memory_space=pltpu.VMEM)
    hbm = pl.BlockSpec(memory_space=pl.ANY)
    dma = pltpu.SemaphoreType.DMA
    apart = weight.transpose(1, 0, 2)
    out = pl.pallas_call(
        functools.partial(exchange, n, ny, lf, wide),
        out_shape=jax.ShapeDtypeStruct((total, lf), jnp.bfloat16),
        in_specs=[vmem] * 5 + [hbm],
        out_specs=vmem,
        scratch_shapes=[
            pltpu.VMEM((n, total, width), jnp.bfloat16),
            pltpu.VMEM((n, 8, 128), jnp.float32),
            pltpu.VMEM((n, 2, block, lf), jnp.bfloat16),
            pltpu.VMEM((n, block, paired), jnp.float32),
            pltpu.VMEM((n, 2, block, lf), jnp.bfloat16),
            pltpu.VMEM((2, n * width, lf), jnp.bfloat16),
            pltpu.VMEM((2, total, lf), jnp.float32),
            dma((4, n, 2)), dma((n, 2)), dma((n,)), dma((n,)), dma((n,)), dma((n,)),
            dma((n,)), dma((n,)), dma((4,)),
        ],
        compiler_params=pltpu.CompilerParams(
            collective_id=0, has_side_effects=True, vmem_limit_bytes=60 * 2**20),
    )(xg, ssq, sp, maps, back, apart)
    return out.reshape(steps, rows, lf)


def solution(mesh):
    return jax.shard_map(
        functools.partial(per_device, mesh.shape["tensor"]),
        mesh=mesh,
        in_specs=(
            P(None, "groups", "tensor"),
            P("tensor"),
            P(None, None, "tensor"),
            P("tensor", None, None),
            P("tensor", None, None, None),
            P(None, "groups", None),
            P(),
        ),
        out_specs=P(None, "groups", "tensor"),
        check_vma=False,
    )
```

```python
import functools
import jax
import jax.numpy as jnp
from jax import lax
from jax.experimental import pallas as pl
from jax.experimental.pallas import tpu as pltpu
from jax.sharding import PartitionSpec as P

CAP = 16
MESH = pl.DeviceIdType.MESH


def exchange(n, ny, lf, wide, xg, ssq, sp, up, back, weight, below, above,
             aside, beside, out, xall, ssq_all,
             lora_all, sp_all, lora_buf, w, acc, x_send, x_recv, q_send, q_recv,
             s_send, s_recv, l_send, l_recv, own_sem):
    nz = n // (2 * ny)
    me = lax.axis_index("tensor")
    core = lax.rem(me, 2)
    y = lax.rem(me // 2, ny)
    z = me // (2 * ny)
    half = up.shape[-2]
    total, width = xg.shape
    part = total // 2

    def index(zz, yy, cc):
        return lax.rem((zz * ny + yy) * 2 + cc + n, n)

    load = pltpu.make_async_copy(weight, w, own_sem.at[2])
    load.start()

    def placed(act):
        if nz > 1:
            @pl.when(z > 0)
            def _():
                act(pltpu.make_async_copy(below, xall.at[index(z - 1, y, core)], own_sem.at[4]))

            @pl.when(z + 1 < nz)
            def _():
                act(pltpu.make_async_copy(above, xall.at[index(z + 1, y, core)], own_sem.at[5]))
        if ny == 2:
            act(pltpu.make_async_copy(aside, xall.at[index(z, 1 - y, core)], own_sem.at[6]))
        act(pltpu.make_async_copy(beside, xall.at[index(z, y, 1 - core)], own_sem.at[7]))

    placed(lambda copy: copy.start())

    barrier = pltpu.get_barrier_semaphore()

    @pl.loop(1, n)
    def _(d):
        pl.semaphore_signal(barrier, inc=1, device_id={"tensor": lax.rem(me + d, n)},
                            device_id_type=MESH)

    pl.semaphore_wait(barrier, n - 1)

    def remote(src, dst, send, recv, peer):
        return pltpu.make_async_remote_copy(
            src_ref=src, dst_ref=dst, send_sem=send, recv_sem=recv,
            device_id={"tensor": peer}, device_id_type=MESH)

    def sp_copy(peer, slot):
        return remote(sp.at[peer], sp_all.at[slot], s_send.at[peer], s_recv.at[slot], peer)

    def ssq_copy(peer, slot):
        return remote(ssq, ssq_all.at[slot], q_send.at[peer], q_recv.at[slot], peer)

    def lora_copy(peer, slot):
        return remote(lora_buf.at[peer], lora_all.at[slot], l_send.at[peer],
                      l_recv.at[slot], peer)

    def rows(h):
        return pl.ds(h * part, part)

    def x_copy(way, block, h, peer):
        return remote(xall.at[block, rows(h)], xall.at[block, rows(h)], x_send.at[way, block, h],
                      x_recv.at[block, h], peer)

    def sends(block, h, act, rising):
        if rising:
            @pl.when(z + 1 < nz)
            def _():
                act(x_copy(0, block, h, index(z + 1, y, core)))
        else:
            @pl.when(z > 0)
            def _():
                act(x_copy(1, block, h, index(z - 1, y, core)))
        if ny == 2:
            act(x_copy(2, block, h, index(z, 1 - y, core)))
        act(x_copy(3, block, h, index(z, y, 1 - core)))

    def landed(block, h):
        x_copy(0, block, h, lax.rem(me + 1, n)).wait_recv()

    def both(step, run):
        @pl.when(z - step >= 0)
        def _():
            run(z - step, True)

        @pl.when(jnp.logical_and(step > 0, z + step < nz))
        def _():
            run(z + step, False)

    def relay(step, act, wait):
        for h in range(2):
            def line(zz, rising):
                block = index(zz, y, core)
                if wait:
                    landed(block, h)
                sends(block, h, act, rising)

            both(step, line)

    def relay_side(step, act, wait):
        for h in range(2):
            def side(zz, rising):
                block = index(zz, 1 - y, core)
                if wait:
                    landed(block, h)
                act(x_copy(3, block, h, index(z, y, 1 - core)))

            both(step, side)

    def use(step, yy, cc, wait):
        def one(zz, rising):
            block = index(zz, yy, cc)
            if wait:
                landed(block, 0)
                landed(block, 1)
            for g in range(2):
                acc[g] += jnp.dot(xall[block], w[g, pl.ds(pl.multiple_of(block * width, 128), width)],
                                  preferred_element_type=jnp.float32)

        both(step, one)

    def begin(copy):
        copy.start()

    def finish(copy):
        copy.wait_send()

    @pl.loop(1, n)
    def _(d):
        sp_copy(lax.rem(me + d, n), me).start()

    placed(lambda copy: copy.wait())
    relay(1, begin, False)
    if ny == 2:
        relay_side(0, begin, False)

    @pl.loop(1, n)
    def _(d):
        ssq_copy(lax.rem(me + d, n), me).start()

    own = [pltpu.make_async_copy(sp.at[me], sp_all.at[me], own_sem.at[0]),
           pltpu.make_async_copy(ssq, ssq_all.at[me], own_sem.at[1])]
    for copy in own:
        copy.start()
    own[0].wait()

    @pl.loop(1, n)
    def _(d):
        peer = lax.rem(me + d, n)
        sp_copy(peer, peer).wait_recv()

    shrink = jnp.sum(sp_all[...], axis=0).astype(jnp.bfloat16)

    @pl.loop(1, n + 1)
    def _(d):
        peer = lax.rem(me + d, n)
        for g in range(2):
            if wide:
                maps = up[0, g, :, pl.ds(pl.multiple_of(peer * lf, 128), lf)]
            else:
                maps = up[peer, g]
            lora_buf[peer, g] = jnp.dot(
                shrink[:, g * half:(g + 1) * half], maps,
                preferred_element_type=jnp.float32).astype(jnp.bfloat16)

        @pl.when(d < n)
        def _():
            lora_copy(peer, me).start()

    mine = pltpu.make_async_copy(lora_buf.at[me], lora_all.at[me], own_sem.at[3])
    mine.start()

    load.wait()
    for g in range(2):
        acc[g] = jnp.dot(xg[...], w[g, pl.ds(pl.multiple_of(me * width, 128), width)],
                         preferred_element_type=jnp.float32)

    use(1, y, core, False)
    use(0, y, 1 - core, False)
    if ny == 2:
        use(0, 1 - y, core, False)

    @pl.loop(2, nz)
    def _(step):
        relay(step, begin, True)
        if ny == 2:
            relay_side(step - 1, begin, True)
        use(step, y, core, False)
        use(step - 1, y, 1 - core, True)
        if ny == 2:
            use(step - 1, 1 - y, core, False)
            use(step - 2, 1 - y, 1 - core, True)

    if ny == 2:
        relay_side(nz - 1, begin, True)
        use(nz - 1, 1 - y, core, False)
        use(nz - 2, 1 - y, 1 - core, True)
    use(nz - 1, y, 1 - core, True)

    @pl.loop(1, n)
    def _(d):
        peer = lax.rem(me + d, n)
        lora_copy(peer, peer).wait_recv()
        ssq_copy(peer, peer).wait_recv()

    own[1].wait()
    mine.wait()
    for g in range(2):
        flat = lora_all[:, g].reshape(back.shape[1], lf)
        acc[g] += 2.0 * jnp.dot(back[...], flat, preferred_element_type=jnp.float32)
    if ny == 2:
        use(nz - 1, 1 - y, 1 - core, True)

    sums = jnp.sum(ssq_all[...], axis=0)
    diagonal = (lax.broadcasted_iota(jnp.int32, (128, 128), 0)
                == lax.broadcasted_iota(jnp.int32, (128, 128), 1))
    for i in range(total // 128):
        line = jnp.broadcast_to(sums[i:i + 1, :], (128, 128))
        column = jnp.sum(jnp.where(diagonal, line, 0.0), axis=1, keepdims=True)
        rstd = lax.rsqrt(column / (width * n) + 1e-05)
        gate = acc[0, i * 128:(i + 1) * 128] * rstd
        upper = acc[1, i * 128:(i + 1) * 128] * rstd
        out[i * 128:(i + 1) * 128, :] = (
            gate / (1.0 + jnp.exp(-gate)) * upper).astype(out.dtype)

    @pl.loop(1, n)
    def _(d):
        peer = lax.rem(me + d, n)
        lora_copy(peer, me).wait_send()
        ssq_copy(peer, me).wait_send()
        sp_copy(peer, me).wait_send()

    @pl.loop(1, nz)
    def _(step):
        relay(step, finish, False)

    if ny == 2:
        @pl.loop(0, nz)
        def _(step):
            relay_side(step, finish, False)


def per_device(n, x, gain, weight, down, up, row_ids, slots):
    steps, rows, width = x.shape
    lf = weight.shape[2]
    total = steps * rows
    adapters, paired = down.shape[1], down.shape[2]
    rank = paired // 2
    block = steps * CAP
    ny = 2 if n == 16 else 1
    flat = x.reshape(total, width).astype(jnp.float32)
    xg = (flat * gain.astype(jnp.float32)[None, :]).astype(jnp.bfloat16)
    ssq = jnp.sum(flat * flat, axis=1).reshape(total // 128, 128)
    ssq = jnp.pad(ssq, ((0, 8 - total // 128), (0, 0)))

    stride = 2 * ny
    pairs = [[(i, i + stride) for i in range(n - stride)],
             [(i + stride, i) for i in range(n - stride)],
             [(i, i ^ 2 if ny == 2 else i ^ 1) for i in range(n)],
             [(i, i ^ 1) for i in range(n)]]
    near = [lax.ppermute(xg, "tensor", perm) for perm in pairs]

    ids = row_ids.reshape(steps, rows)
    earlier = jnp.arange(rows)[None, :] < jnp.arange(rows)[:, None]
    same = jnp.logical_and(ids[:, :, None] == ids[:, None, :], earlier[None])
    place = jnp.sum(same.astype(jnp.int32), axis=2) + CAP * jnp.arange(steps, dtype=jnp.int32)[:, None]
    place = place.reshape(total)
    ids = ids.reshape(total)
    hot = ids[:, None] == jnp.arange(adapters, dtype=jnp.int32)[None, :]
    slot = jnp.sum(jnp.where(hot, slots[None, :], 0), axis=1)
    spots = jnp.arange(adapters * block, dtype=jnp.int32)
    out_map = (spots[:, None] == (ids * block + place)[None, :]).astype(jnp.bfloat16)
    back = ((slot * block + place)[:, None] == spots[None, :]).astype(jnp.bfloat16)
    sent = jnp.dot(out_map, xg, preferred_element_type=jnp.float32).astype(jnp.bfloat16)
    sp = jnp.einsum("apk,kac->apc", sent.reshape(adapters, block, width), down,
                    preferred_element_type=jnp.float32)
    order = (jnp.arange(adapters, dtype=jnp.int32)[:, None] == slots[None, :]).astype(jnp.float32)
    sp = jnp.einsum("ta,apc->tpc", order, sp, precision=lax.Precision.HIGHEST)

    wide = lf % 128 == 0
    maps = up if wide else up.reshape(2, rank, n, lf).transpose(2, 0, 1, 3)
    vmem = pl.BlockSpec(memory_space=pltpu.VMEM)
    hbm = pl.BlockSpec(memory_space=pl.ANY)
    dma = pltpu.SemaphoreType.DMA
    apart = weight.transpose(1, 0, 2)
    out = pl.pallas_call(
        functools.partial(exchange, n, ny, lf, wide),
        out_shape=jax.ShapeDtypeStruct((total, lf), jnp.bfloat16),
        in_specs=[vmem] * 5 + [hbm] * 5,
        out_specs=vmem,
        scratch_shapes=[
            pltpu.VMEM((n, total, width), jnp.bfloat16),
            pltpu.VMEM((n, 8, 128), jnp.float32),
            pltpu.VMEM((n, 2, block, lf), jnp.bfloat16),
            pltpu.VMEM((n, block, paired), jnp.float32),
            pltpu.VMEM((n, 2, block, lf), jnp.bfloat16),
            pltpu.VMEM((2, n * width, lf), jnp.bfloat16),
            pltpu.VMEM((2, total, lf), jnp.float32),
            dma((4, n, 2)), dma((n, 2)), dma((n,)), dma((n,)), dma((n,)), dma((n,)),
            dma((n,)), dma((n,)), dma((8,)),
        ],
        compiler_params=pltpu.CompilerParams(
            collective_id=0, has_side_effects=True, vmem_limit_bytes=60 * 2**20),
    )(xg, ssq, sp, maps, back, apart, *near)
    return out.reshape(steps, rows, lf)


def solution(mesh):
    return jax.shard_map(
        functools.partial(per_device, mesh.shape["tensor"]),
        mesh=mesh,
        in_specs=(
            P(None, "groups", "tensor"),
            P("tensor"),
            P(None, None, "tensor"),
            P("tensor", None, None),
            P("tensor", None, None, None),
            P(None, "groups", None),
            P(),
        ),
        out_specs=P(None, "groups", "tensor"),
        check_vma=False,
    )
```

```python
import functools
import jax
import jax.numpy as jnp
from jax import lax
from jax.experimental import pallas as pl
from jax.experimental.pallas import tpu as pltpu
from jax.sharding import PartitionSpec as P

CAP = 16
MESH = pl.DeviceIdType.MESH


def exchange(n, ny, lf, wide, xg, ssq, sp, up, back, weight, below, above,
             aside, beside, out, xall, ssq_all,
             lora_all, sp_all, lora_buf, w, acc, x_send, x_recv, q_send, q_recv,
             s_send, s_recv, l_send, l_recv, own_sem):
    nz = n // (2 * ny)
    me = lax.axis_index("tensor")
    core = lax.rem(me, 2)
    y = lax.rem(me // 2, ny)
    z = me // (2 * ny)
    half = up.shape[-2]
    total, width = xg.shape
    part = total // 2

    def index(zz, yy, cc):
        return lax.rem((zz * ny + yy) * 2 + cc + n, n)

    load = pltpu.make_async_copy(weight, w, own_sem.at[2])
    load.start()

    def placed(act):
        if nz > 1:
            @pl.when(z > 0)
            def _():
                act(pltpu.make_async_copy(below, xall.at[index(z - 1, y, core)], own_sem.at[4]))

            @pl.when(z + 1 < nz)
            def _():
                act(pltpu.make_async_copy(above, xall.at[index(z + 1, y, core)], own_sem.at[5]))
        if ny == 2:
            act(pltpu.make_async_copy(aside, xall.at[index(z, 1 - y, core)], own_sem.at[6]))
        act(pltpu.make_async_copy(beside, xall.at[index(z, y, 1 - core)], own_sem.at[7]))

    placed(lambda copy: copy.start())

    barrier = pltpu.get_barrier_semaphore()

    @pl.loop(1, n)
    def _(d):
        pl.semaphore_signal(barrier, inc=1, device_id={"tensor": lax.rem(me + d, n)},
                            device_id_type=MESH)

    pl.semaphore_wait(barrier, n - 1)

    def remote(src, dst, send, recv, peer):
        return pltpu.make_async_remote_copy(
            src_ref=src, dst_ref=dst, send_sem=send, recv_sem=recv,
            device_id={"tensor": peer}, device_id_type=MESH)

    def sp_copy(peer, slot):
        return remote(sp.at[peer], sp_all.at[slot], s_send.at[peer], s_recv.at[slot], peer)

    def ssq_copy(peer, slot):
        return remote(ssq, ssq_all.at[slot], q_send.at[peer], q_recv.at[slot], peer)

    def lora_copy(peer, slot):
        return remote(lora_buf.at[peer], lora_all.at[slot], l_send.at[peer],
                      l_recv.at[slot], peer)

    def rows(h):
        return pl.ds(h * part, part)

    def x_copy(way, block, h, peer):
        return remote(xall.at[block, rows(h)], xall.at[block, rows(h)], x_send.at[way, block, h],
                      x_recv.at[block, h], peer)

    def sends(block, h, act, rising):
        if rising:
            @pl.when(z + 1 < nz)
            def _():
                act(x_copy(0, block, h, index(z + 1, y, core)))
        else:
            @pl.when(z > 0)
            def _():
                act(x_copy(1, block, h, index(z - 1, y, core)))
        if ny == 2:
            act(x_copy(2, block, h, index(z, 1 - y, core)))
        act(x_copy(3, block, h, index(z, y, 1 - core)))

    def landed(block, h):
        x_copy(0, block, h, lax.rem(me + 1, n)).wait_recv()

    def both(step, run):
        @pl.when(z - step >= 0)
        def _():
            run(z - step, True)

        @pl.when(jnp.logical_and(step > 0, z + step < nz))
        def _():
            run(z + step, False)

    def relay(step, act, wait):
        for h in range(2):
            def line(zz, rising):
                block = index(zz, y, core)
                if wait:
                    landed(block, h)
                sends(block, h, act, rising)

            both(step, line)

    def relay_side(step, act, wait):
        for h in range(2):
            def side(zz, rising):
                block = index(zz, 1 - y, core)
                if wait:
                    landed(block, h)
                act(x_copy(3, block, h, index(z, y, 1 - core)))

            both(step, side)

    def use(step, yy, cc, wait):
        def one(zz, rising):
            block = index(zz, yy, cc)
            if wait:
                landed(block, 0)
                landed(block, 1)
            for g in range(2):
                acc[g] += jnp.dot(xall[block], w[g, pl.ds(pl.multiple_of(block * width, 128), width)],
                                  preferred_element_type=jnp.float32)

        both(step, one)

    def begin(copy):
        copy.start()

    def finish(copy):
        copy.wait_send()

    @pl.loop(1, n)
    def _(d):
        sp_copy(lax.rem(me + d, n), me).start()

    placed(lambda copy: copy.wait())
    relay(1, begin, False)
    if ny == 2:
        relay_side(0, begin, False)

    @pl.loop(1, n)
    def _(d):
        ssq_copy(lax.rem(me + d, n), me).start()

    own = [pltpu.make_async_copy(sp.at[me], sp_all.at[me], own_sem.at[0]),
           pltpu.make_async_copy(ssq, ssq_all.at[me], own_sem.at[1])]
    for copy in own:
        copy.start()
    own[0].wait()

    @pl.loop(1, n)
    def _(d):
        peer = lax.rem(me + d, n)
        sp_copy(peer, peer).wait_recv()

    shrink = jnp.sum(sp_all[...], axis=0).astype(jnp.bfloat16)

    @pl.loop(1, n + 1)
    def _(d):
        peer = lax.rem(me + d, n)
        for g in range(2):
            if wide:
                maps = up[0, g, :, pl.ds(pl.multiple_of(peer * lf, 128), lf)]
            else:
                maps = up[peer, g]
            lora_buf[peer, g] = jnp.dot(
                shrink[:, g * half:(g + 1) * half], maps,
                preferred_element_type=jnp.float32).astype(jnp.bfloat16)

        @pl.when(d < n)
        def _():
            lora_copy(peer, me).start()

    mine = pltpu.make_async_copy(lora_buf.at[me], lora_all.at[me], own_sem.at[3])
    mine.start()

    relay(2, begin, True)
    if ny == 2:
        relay_side(1, begin, True)

    load.wait()
    for g in range(2):
        acc[g] = jnp.dot(xg[...], w[g, pl.ds(pl.multiple_of(me * width, 128), width)],
                         preferred_element_type=jnp.float32)

    use(1, y, core, False)
    use(0, y, 1 - core, False)
    if ny == 2:
        use(0, 1 - y, core, False)

    @pl.loop(3, nz)
    def _(step):
        relay(step, begin, True)
        if ny == 2:
            relay_side(step - 1, begin, True)
        use(step - 1, y, core, False)
        use(step - 2, y, 1 - core, True)
        if ny == 2:
            use(step - 2, 1 - y, core, False)
            use(step - 3, 1 - y, 1 - core, True)

    if ny == 2:
        relay_side(nz - 1, begin, True)
    use(nz - 1, y, core, False)
    use(nz - 2, y, 1 - core, True)
    if ny == 2:
        use(nz - 2, 1 - y, core, False)
        use(nz - 3, 1 - y, 1 - core, True)
        use(nz - 1, 1 - y, core, False)
        use(nz - 2, 1 - y, 1 - core, True)
    use(nz - 1, y, 1 - core, True)

    @pl.loop(1, n)
    def _(d):
        peer = lax.rem(me + d, n)
        lora_copy(peer, peer).wait_recv()
        ssq_copy(peer, peer).wait_recv()

    own[1].wait()
    mine.wait()
    for g in range(2):
        flat = lora_all[:, g].reshape(back.shape[1], lf)
        acc[g] += 2.0 * jnp.dot(back[...], flat, preferred_element_type=jnp.float32)
    if ny == 2:
        use(nz - 1, 1 - y, 1 - core, True)

    sums = jnp.sum(ssq_all[...], axis=0)
    diagonal = (lax.broadcasted_iota(jnp.int32, (128, 128), 0)
                == lax.broadcasted_iota(jnp.int32, (128, 128), 1))
    for i in range(total // 128):
        line = jnp.broadcast_to(sums[i:i + 1, :], (128, 128))
        column = jnp.sum(jnp.where(diagonal, line, 0.0), axis=1, keepdims=True)
        rstd = lax.rsqrt(column / (width * n) + 1e-05)
        gate = acc[0, i * 128:(i + 1) * 128] * rstd
        upper = acc[1, i * 128:(i + 1) * 128] * rstd
        out[i * 128:(i + 1) * 128, :] = (
            gate / (1.0 + jnp.exp(-gate)) * upper).astype(out.dtype)

    @pl.loop(1, n)
    def _(d):
        peer = lax.rem(me + d, n)
        lora_copy(peer, me).wait_send()
        ssq_copy(peer, me).wait_send()
        sp_copy(peer, me).wait_send()

    @pl.loop(1, nz)
    def _(step):
        relay(step, finish, False)

    if ny == 2:
        @pl.loop(0, nz)
        def _(step):
            relay_side(step, finish, False)


def per_device(n, x, gain, weight, down, up, row_ids, slots):
    steps, rows, width = x.shape
    lf = weight.shape[2]
    total = steps * rows
    adapters, paired = down.shape[1], down.shape[2]
    rank = paired // 2
    block = steps * CAP
    ny = 2 if n == 16 else 1
    flat = x.reshape(total, width).astype(jnp.float32)
    xg = (flat * gain.astype(jnp.float32)[None, :]).astype(jnp.bfloat16)
    ssq = jnp.sum(flat * flat, axis=1).reshape(total // 128, 128)
    ssq = jnp.pad(ssq, ((0, 8 - total // 128), (0, 0)))

    stride = 2 * ny
    pairs = [[(i, i + stride) for i in range(n - stride)],
             [(i + stride, i) for i in range(n - stride)],
             [(i, i ^ 2 if ny == 2 else i ^ 1) for i in range(n)],
             [(i, i ^ 1) for i in range(n)]]
    near = [lax.ppermute(xg, "tensor", perm) for perm in pairs]

    ids = row_ids.reshape(steps, rows)
    earlier = jnp.arange(rows)[None, :] < jnp.arange(rows)[:, None]
    same = jnp.logical_and(ids[:, :, None] == ids[:, None, :], earlier[None])
    place = jnp.sum(same.astype(jnp.int32), axis=2) + CAP * jnp.arange(steps, dtype=jnp.int32)[:, None]
    place = place.reshape(total)
    ids = ids.reshape(total)
    hot = ids[:, None] == jnp.arange(adapters, dtype=jnp.int32)[None, :]
    slot = jnp.sum(jnp.where(hot, slots[None, :], 0), axis=1)
    spots = jnp.arange(adapters * block, dtype=jnp.int32)
    out_map = (spots[:, None] == (ids * block + place)[None, :]).astype(jnp.bfloat16)
    back = ((slot * block + place)[:, None] == spots[None, :]).astype(jnp.bfloat16)
    sent = jnp.dot(out_map, xg, preferred_element_type=jnp.float32).astype(jnp.bfloat16)
    sp = jnp.einsum("apk,kac->apc", sent.reshape(adapters, block, width), down,
                    preferred_element_type=jnp.float32)
    order = (jnp.arange(adapters, dtype=jnp.int32)[:, None] == slots[None, :]).astype(jnp.float32)
    sp = jnp.einsum("ta,apc->tpc", order, sp, precision=lax.Precision.HIGHEST)

    wide = lf % 128 == 0
    maps = up if wide else up.reshape(2, rank, n, lf).transpose(2, 0, 1, 3)
    vmem = pl.BlockSpec(memory_space=pltpu.VMEM)
    hbm = pl.BlockSpec(memory_space=pl.ANY)
    dma = pltpu.SemaphoreType.DMA
    apart = weight.transpose(1, 0, 2)
    out = pl.pallas_call(
        functools.partial(exchange, n, ny, lf, wide),
        out_shape=jax.ShapeDtypeStruct((total, lf), jnp.bfloat16),
        in_specs=[vmem] * 5 + [hbm] * 5,
        out_specs=vmem,
        scratch_shapes=[
            pltpu.VMEM((n, total, width), jnp.bfloat16),
            pltpu.VMEM((n, 8, 128), jnp.float32),
            pltpu.VMEM((n, 2, block, lf), jnp.bfloat16),
            pltpu.VMEM((n, block, paired), jnp.float32),
            pltpu.VMEM((n, 2, block, lf), jnp.bfloat16),
            pltpu.VMEM((2, n * width, lf), jnp.bfloat16),
            pltpu.VMEM((2, total, lf), jnp.float32),
            dma((4, n, 2)), dma((n, 2)), dma((n,)), dma((n,)), dma((n,)), dma((n,)),
            dma((n,)), dma((n,)), dma((8,)),
        ],
        compiler_params=pltpu.CompilerParams(
            collective_id=0, has_side_effects=True, vmem_limit_bytes=60 * 2**20),
    )(xg, ssq, sp, maps, back, apart, *near)
    return out.reshape(steps, rows, lf)


def solution(mesh):
    return jax.shard_map(
        functools.partial(per_device, mesh.shape["tensor"]),
        mesh=mesh,
        in_specs=(
            P(None, "groups", "tensor"),
            P("tensor"),
            P(None, None, "tensor"),
            P("tensor", None, None),
            P("tensor", None, None, None),
            P(None, "groups", None),
            P(),
        ),
        out_specs=P(None, "groups", "tensor"),
        check_vma=False,
    )
```

```python
import functools
import jax
import jax.numpy as jnp
from jax import lax
from jax.experimental import pallas as pl
from jax.experimental.pallas import tpu as pltpu
from jax.sharding import PartitionSpec as P

CAP = 16
MESH = pl.DeviceIdType.MESH


def exchange(n, ny, lf, wide, xg, ssq, sp, up, back, weight, below, above,
             aside, beside, out, xall, ssq_all,
             lora_all, sp_all, lora_buf, w, acc, x_send, x_recv, q_send, q_recv,
             s_send, s_recv, l_send, l_recv, own_sem):
    nz = n // (2 * ny)
    me = lax.axis_index("tensor")
    core = lax.rem(me, 2)
    y = lax.rem(me // 2, ny)
    z = me // (2 * ny)
    half = up.shape[-2]
    total, width = xg.shape
    part = total // 2

    def index(zz, yy, cc):
        return lax.rem((zz * ny + yy) * 2 + cc + n, n)

    load = pltpu.make_async_copy(weight, w, own_sem.at[2])
    load.start()

    def placed(act):
        if nz > 1:
            @pl.when(z > 0)
            def _():
                act(pltpu.make_async_copy(below, xall.at[index(z - 1, y, core)], own_sem.at[4]))

            @pl.when(z + 1 < nz)
            def _():
                act(pltpu.make_async_copy(above, xall.at[index(z + 1, y, core)], own_sem.at[5]))
        if ny == 2:
            act(pltpu.make_async_copy(aside, xall.at[index(z, 1 - y, core)], own_sem.at[6]))
        act(pltpu.make_async_copy(beside, xall.at[index(z, y, 1 - core)], own_sem.at[7]))

    placed(lambda copy: copy.start())

    barrier = pltpu.get_barrier_semaphore()

    @pl.loop(1, n)
    def _(d):
        pl.semaphore_signal(barrier, inc=1, device_id={"tensor": lax.rem(me + d, n)},
                            device_id_type=MESH)

    pl.semaphore_wait(barrier, n - 1)

    def remote(src, dst, send, recv, peer):
        return pltpu.make_async_remote_copy(
            src_ref=src, dst_ref=dst, send_sem=send, recv_sem=recv,
            device_id={"tensor": peer}, device_id_type=MESH)

    def sp_copy(peer, slot):
        return remote(sp.at[peer], sp_all.at[slot], s_send.at[peer], s_recv.at[slot], peer)

    def ssq_copy(peer, slot):
        return remote(ssq, ssq_all.at[slot], q_send.at[peer], q_recv.at[slot], peer)

    def lora_copy(peer, slot):
        return remote(lora_buf.at[peer], lora_all.at[slot], l_send.at[peer],
                      l_recv.at[slot], peer)

    def rows(h):
        return pl.ds(h * part, part)

    def x_copy(way, block, h, peer):
        return remote(xall.at[block, rows(h)], xall.at[block, rows(h)], x_send.at[way, block, h],
                      x_recv.at[block, h], peer)

    def sends(block, h, act, rising):
        if rising:
            @pl.when(z + 1 < nz)
            def _():
                act(x_copy(0, block, h, index(z + 1, y, core)))
        else:
            @pl.when(z > 0)
            def _():
                act(x_copy(1, block, h, index(z - 1, y, core)))
        if ny == 2:
            act(x_copy(2, block, h, index(z, 1 - y, core)))
        act(x_copy(3, block, h, index(z, y, 1 - core)))

    def landed(block, h):
        x_copy(0, block, h, lax.rem(me + 1, n)).wait_recv()

    def both(step, run):
        @pl.when(z - step >= 0)
        def _():
            run(z - step, True)

        @pl.when(jnp.logical_and(step > 0, z + step < nz))
        def _():
            run(z + step, False)

    def relay(step, act, wait):
        for h in range(2):
            def line(zz, rising):
                block = index(zz, y, core)
                if wait:
                    landed(block, h)
                sends(block, h, act, rising)

            both(step, line)

    def relay_side(step, act, wait):
        for h in range(2):
            def side(zz, rising):
                block = index(zz, 1 - y, core)
                if wait:
                    landed(block, h)
                act(x_copy(3, block, h, index(z, y, 1 - core)))

            both(step, side)

    def use(step, yy, cc, wait):
        def one(zz, rising):
            block = index(zz, yy, cc)
            if wait:
                landed(block, 0)
                landed(block, 1)
            for g in range(2):
                acc[g] += jnp.dot(xall[block], w[g, pl.ds(pl.multiple_of(block * width, 128), width)],
                                  preferred_element_type=jnp.float32)

        both(step, one)

    def begin(copy):
        copy.start()

    def finish(copy):
        copy.wait_send()

    @pl.loop(1, n)
    def _(d):
        sp_copy(lax.rem(me + d, n), me).start()

    placed(lambda copy: copy.wait())
    relay(1, begin, False)
    if ny == 2:
        relay_side(0, begin, False)

    @pl.loop(1, n)
    def _(d):
        ssq_copy(lax.rem(me + d, n), me).start()

    own = [pltpu.make_async_copy(sp.at[me], sp_all.at[me], own_sem.at[0]),
           pltpu.make_async_copy(ssq, ssq_all.at[me], own_sem.at[1])]
    for copy in own:
        copy.start()
    own[0].wait()

    load.wait()
    for g in range(2):
        acc[g] = jnp.dot(xg[...], w[g, pl.ds(pl.multiple_of(me * width, 128), width)],
                         preferred_element_type=jnp.float32)

    @pl.loop(1, n)
    def _(d):
        peer = lax.rem(me + d, n)
        sp_copy(peer, peer).wait_recv()

    shrink = jnp.sum(sp_all[...], axis=0).astype(jnp.bfloat16)

    @pl.loop(1, n + 1)
    def _(d):
        peer = lax.rem(me + d, n)
        for g in range(2):
            if wide:
                maps = up[0, g, :, pl.ds(pl.multiple_of(peer * lf, 128), lf)]
            else:
                maps = up[peer, g]
            lora_buf[peer, g] = jnp.dot(
                shrink[:, g * half:(g + 1) * half], maps,
                preferred_element_type=jnp.float32).astype(jnp.bfloat16)

        @pl.when(d < n)
        def _():
            lora_copy(peer, me).start()

    mine = pltpu.make_async_copy(lora_buf.at[me], lora_all.at[me], own_sem.at[3])
    mine.start()

    use(1, y, core, False)
    use(0, y, 1 - core, False)
    if ny == 2:
        use(0, 1 - y, core, False)

    @pl.loop(2, nz)
    def _(step):
        relay(step, begin, True)
        if ny == 2:
            relay_side(step - 1, begin, True)
        use(step, y, core, False)
        use(step - 1, y, 1 - core, True)
        if ny == 2:
            use(step - 1, 1 - y, core, False)
            use(step - 2, 1 - y, 1 - core, True)

    if ny == 2:
        relay_side(nz - 1, begin, True)
        use(nz - 1, 1 - y, core, False)
        use(nz - 2, 1 - y, 1 - core, True)
    use(nz - 1, y, 1 - core, True)

    @pl.loop(1, n)
    def _(d):
        peer = lax.rem(me + d, n)
        lora_copy(peer, peer).wait_recv()
        ssq_copy(peer, peer).wait_recv()

    own[1].wait()
    mine.wait()
    for g in range(2):
        flat = lora_all[:, g].reshape(back.shape[1], lf)
        acc[g] += 2.0 * jnp.dot(back[...], flat, preferred_element_type=jnp.float32)
    if ny == 2:
        use(nz - 1, 1 - y, 1 - core, True)

    sums = jnp.sum(ssq_all[...], axis=0)
    diagonal = (lax.broadcasted_iota(jnp.int32, (128, 128), 0)
                == lax.broadcasted_iota(jnp.int32, (128, 128), 1))
    for i in range(total // 128):
        line = jnp.broadcast_to(sums[i:i + 1, :], (128, 128))
        column = jnp.sum(jnp.where(diagonal, line, 0.0), axis=1, keepdims=True)
        rstd = lax.rsqrt(column / (width * n) + 1e-05)
        gate = acc[0, i * 128:(i + 1) * 128] * rstd
        upper = acc[1, i * 128:(i + 1) * 128] * rstd
        out[i * 128:(i + 1) * 128, :] = (
            gate / (1.0 + jnp.exp(-gate)) * upper).astype(out.dtype)

    @pl.loop(1, n)
    def _(d):
        peer = lax.rem(me + d, n)
        lora_copy(peer, me).wait_send()
        ssq_copy(peer, me).wait_send()
        sp_copy(peer, me).wait_send()

    @pl.loop(1, nz)
    def _(step):
        relay(step, finish, False)

    if ny == 2:
        @pl.loop(0, nz)
        def _(step):
            relay_side(step, finish, False)


def per_device(n, x, gain, weight, down, up, row_ids, slots):
    steps, rows, width = x.shape
    lf = weight.shape[2]
    total = steps * rows
    adapters, paired = down.shape[1], down.shape[2]
    rank = paired // 2
    block = steps * CAP
    ny = 2 if n == 16 else 1
    flat = x.reshape(total, width).astype(jnp.float32)
    xg = (flat * gain.astype(jnp.float32)[None, :]).astype(jnp.bfloat16)
    ssq = jnp.sum(flat * flat, axis=1).reshape(total // 128, 128)
    ssq = jnp.pad(ssq, ((0, 8 - total // 128), (0, 0)))

    stride = 2 * ny
    pairs = [[(i, i + stride) for i in range(n - stride)],
             [(i + stride, i) for i in range(n - stride)],
             [(i, i ^ 2 if ny == 2 else i ^ 1) for i in range(n)],
             [(i, i ^ 1) for i in range(n)]]
    near = [lax.ppermute(xg, "tensor", perm) for perm in pairs]

    ids = row_ids.reshape(steps, rows)
    earlier = jnp.arange(rows)[None, :] < jnp.arange(rows)[:, None]
    same = jnp.logical_and(ids[:, :, None] == ids[:, None, :], earlier[None])
    place = jnp.sum(same.astype(jnp.int32), axis=2) + CAP * jnp.arange(steps, dtype=jnp.int32)[:, None]
    place = place.reshape(total)
    ids = ids.reshape(total)
    hot = ids[:, None] == jnp.arange(adapters, dtype=jnp.int32)[None, :]
    slot = jnp.sum(jnp.where(hot, slots[None, :], 0), axis=1)
    spots = jnp.arange(adapters * block, dtype=jnp.int32)
    out_map = (spots[:, None] == (ids * block + place)[None, :]).astype(jnp.bfloat16)
    back = ((slot * block + place)[:, None] == spots[None, :]).astype(jnp.bfloat16)
    sent = jnp.dot(out_map, xg, preferred_element_type=jnp.float32).astype(jnp.bfloat16)
    sp = jnp.einsum("apk,kac->apc", sent.reshape(adapters, block, width), down,
                    preferred_element_type=jnp.float32)
    order = (jnp.arange(adapters, dtype=jnp.int32)[:, None] == slots[None, :]).astype(jnp.float32)
    sp = jnp.einsum("ta,apc->tpc", order, sp, precision=lax.Precision.HIGHEST)

    wide = lf % 128 == 0
    maps = up if wide else up.reshape(2, rank, n, lf).transpose(2, 0, 1, 3)
    vmem = pl.BlockSpec(memory_space=pltpu.VMEM)
    hbm = pl.BlockSpec(memory_space=pl.ANY)
    dma = pltpu.SemaphoreType.DMA
    apart = weight.transpose(1, 0, 2)
    out = pl.pallas_call(
        functools.partial(exchange, n, ny, lf, wide),
        out_shape=jax.ShapeDtypeStruct((total, lf), jnp.bfloat16),
        in_specs=[vmem] * 5 + [hbm] * 5,
        out_specs=vmem,
        scratch_shapes=[
            pltpu.VMEM((n, total, width), jnp.bfloat16),
            pltpu.VMEM((n, 8, 128), jnp.float32),
            pltpu.VMEM((n, 2, block, lf), jnp.bfloat16),
            pltpu.VMEM((n, block, paired), jnp.float32),
            pltpu.VMEM((n, 2, block, lf), jnp.bfloat16),
            pltpu.VMEM((2, n * width, lf), jnp.bfloat16),
            pltpu.VMEM((2, total, lf), jnp.float32),
            dma((4, n, 2)), dma((n, 2)), dma((n,)), dma((n,)), dma((n,)), dma((n,)),
            dma((n,)), dma((n,)), dma((8,)),
        ],
        compiler_params=pltpu.CompilerParams(
            collective_id=0, has_side_effects=True, vmem_limit_bytes=60 * 2**20),
    )(xg, ssq, sp, maps, back, apart, *near)
    return out.reshape(steps, rows, lf)


def solution(mesh):
    return jax.shard_map(
        functools.partial(per_device, mesh.shape["tensor"]),
        mesh=mesh,
        in_specs=(
            P(None, "groups", "tensor"),
            P("tensor"),
            P(None, None, "tensor"),
            P("tensor", None, None),
            P("tensor", None, None, None),
            P(None, "groups", None),
            P(),
        ),
        out_specs=P(None, "groups", "tensor"),
        check_vma=False,
    )
```
